128 devices in a mesh: blk: 8 (over z, y_hi), dp: 16 (over x, y_lo, core).
Axes of the slice: x: 4, y: 4 (y_hi: 2, y_lo: 2; y = y_hi * 2 + y_lo), z: 4, core: 2. Of those that a mesh axis runs over, the one named last changes fastest.
Arguments:
- query_states: bfloat16 [16, 1024, 2560], P('dp', 'blk'), may hold values from -6 to 6
- key_states: bfloat16 [16, 1024, 2560], P('dp', 'blk'), may hold values from -6 to 6
- value_states: bfloat16 [16, 1024, 2560], P('dp', 'blk'), may hold values from -6 to 6
- mask_index: int32 [16, 512], P('dp', 'blk'), may hold values from 0 to 1023, as said below
- cotangent: bfloat16 [16, 512, 4096], P('dp', 'blk'), may hold values from -6 to 6
- out_weight: bfloat16 [2560, 4096], replicated, may hold values from -0.125 to 0.125
Outputs:
- query_grad: bfloat16 [16, 1024, 2560], P('dp', 'blk')
- key_grad: bfloat16 [16, 1024, 2560], P('dp', 'blk')
- value_grad: bfloat16 [16, 1024, 2560], P('dp', 'blk')
- weight_grad: float32 [2560, 4096], P(('blk', 'dp'))
The draws below stay inside these ranges and needn't reach their ends.
Inputs may be any that keep to these rules, and one draw needn't show every extreme that they name: Within each record, entries b * 64 to (b + 1) * 64 - 1 are 64 distinct time steps of the aligned block b * 128 to (b + 1) * 128 - 1, in increasing order; cotangent row i belongs to time step mask_index[r, i].
All inputs are finite; a program needn't handle non-finite values.
Results may differ from the reference program's by a relative error of at most 0.035.
Values may be sent and summed in bfloat16 or wider, within the bound.
No kernel may reach another device: no remote copies, remote signals or barrier semaphores. Data moves between devices by JAX's collectives and lax.ppermute only.
A program may use at most 192 MiB of HBM per device.

```python
import math
import jax
import jax.numpy as jnp
from jax import lax

D = 4096
HEADS = 20
HEAD_DIM = 128
TOK_DEV = 128
HH = 2560
MASKED = 64
LENGTH = 1024
MASKED_ALL = 512
RECORDS = 16


def draw_query_states(key, part):
    key = jax.random.fold_in(key, 11)
    shape = (RECORDS, LENGTH, HEADS * HEAD_DIM)
    base = jnp.clip(jax.random.normal(key, shape, jnp.float32), -6.0, 6.0)
    return base.astype(jnp.bfloat16)


def draw_key_states(key, part):
    key = jax.random.fold_in(key, 17)
    shape = (RECORDS, LENGTH, HEADS * HEAD_DIM)
    base = jnp.clip(jax.random.normal(key, shape, jnp.float32), -6.0, 6.0)
    return base.astype(jnp.bfloat16)


def draw_mask_index(key, part):
    key = jax.random.fold_in(key, 23)
    block_count = LENGTH // TOK_DEV
    ranks = jax.random.randint(key, (RECORDS, block_count, TOK_DEV), 0, 2 ** 20)
    ranks = ranks * TOK_DEV + jnp.arange(TOK_DEV, dtype=jnp.int32)[None, None, :]
    order = jnp.argsort(ranks, axis=-1).astype(jnp.int32)
    picked = jnp.sort(order[:, :, :MASKED], axis=-1)
    offsets = (jnp.arange(block_count, dtype=jnp.int32) * TOK_DEV)[None, :, None]
    return (picked + offsets).reshape(RECORDS, block_count * MASKED).astype(jnp.int32)


def level_of(own_key, shape, cuts, low, largest):
    level, own = 1.0, jax.random.fold_in(own_key, 6)
    for position, blocks in cuts:
        draws = jnp.exp(jax.random.uniform(jax.random.fold_in(own, position), (blocks,), jnp.float32, low / len(cuts), largest / len(cuts)))
        level = level * jnp.repeat(draws, shape[position] // blocks).reshape([-1 if axis == position else 1 for axis in range(len(shape))])
    return level


def normal_values(rng, dims, spread, bound, cuts=(), kind=jnp.bfloat16):
    values = spread * jax.random.normal(rng, dims, jnp.float32)
    if cuts:
        values = values * level_of(rng, dims, cuts, -0.22, 0.18)
    return jnp.clip(values, -bound, bound).astype(kind)


def setup_inputs(seed: int = 0) -> dict:
    arg_keys = jax.random.split(jax.random.key(seed), 7)
    query_states = draw_query_states(jax.random.fold_in(arg_keys[6], 71), 0)
    key_states = draw_key_states(jax.random.fold_in(arg_keys[6], 71), 0)
    value_states = normal_values(arg_keys[2], (RECORDS, LENGTH, HH), 1.0, 6.0, ((0, 16), (1, 8)))
    mask_index = draw_mask_index(jax.random.fold_in(arg_keys[6], 71), 0)
    cotangent = normal_values(arg_keys[4], (RECORDS, MASKED_ALL, D), 1.0, 6.0, ((0, 16), (1, 8)))
    out_weight = normal_values(arg_keys[5], (HH, D), HH ** -0.5, 0.125)
    return dict(query_states=query_states, key_states=key_states, value_states=value_states, mask_index=mask_index, cotangent=cotangent, out_weight=out_weight)


def one_record(query_rec, key_rec, value_rec, mask_rec, cot_rec, out_weight):
    score_scale = 1.0 / math.sqrt(HEAD_DIM)
    length = query_rec.shape[0]
    query_heads = query_rec.astype(jnp.float32).reshape(length, HEADS, HEAD_DIM)
    key_heads = key_rec.astype(jnp.float32).reshape(length, HEADS, HEAD_DIM)
    value_heads = value_rec.astype(jnp.float32).reshape(length, HEADS, HEAD_DIM)
    scores = jnp.einsum('qhd,khd->hqk', query_heads, key_heads) * score_scale
    row_max = lax.optimization_barrier(jnp.max(scores, axis=-1, keepdims=True))
    log_total = row_max + jnp.log(lax.optimization_barrier(jnp.sum(jnp.exp(scores - row_max), axis=-1, keepdims=True)))
    attn_probs = jnp.exp(scores - log_total).astype(jnp.bfloat16)
    attended = jnp.einsum('hqk,khd->qhd', attn_probs.astype(jnp.float32), value_heads).astype(jnp.bfloat16)
    attended = attended.reshape(length, HEADS * HEAD_DIM)
    masked_grad = jnp.dot(cot_rec, out_weight.T, preferred_element_type=jnp.float32).astype(jnp.bfloat16)
    attended_grad = jnp.zeros((length, HEADS * HEAD_DIM), jnp.bfloat16).at[mask_rec].set(masked_grad)
    grad_heads = attended_grad.astype(jnp.float32).reshape(length, HEADS, HEAD_DIM)
    row_delta = lax.optimization_barrier(jnp.sum(grad_heads * attended.astype(jnp.float32).reshape(length, HEADS, HEAD_DIM), axis=-1))
    prob_grad = jnp.einsum('qhd,khd->hqk', grad_heads, value_heads)
    score_grad = (attn_probs.astype(jnp.float32) * (prob_grad - row_delta.T[:, :, None])).astype(jnp.bfloat16)
    score_grad = score_grad.astype(jnp.float32)
    query_grad = (jnp.einsum('hqk,khd->qhd', score_grad, key_heads) * score_scale).astype(jnp.bfloat16)
    key_grad = (jnp.einsum('hqk,qhd->khd', score_grad, query_heads) * score_scale).astype(jnp.bfloat16)
    value_grad = jnp.einsum('hqk,qhd->khd', attn_probs.astype(jnp.float32), grad_heads).astype(jnp.bfloat16)
    attended_masked = attended[mask_rec]
    weight_term = jnp.dot(attended_masked.T, cot_rec, preferred_element_type=jnp.float32)
    shape_out = (length, HEADS * HEAD_DIM)
    return (query_grad.reshape(shape_out), key_grad.reshape(shape_out), value_grad.reshape(shape_out), weight_term)

def reference(query_states, key_states, value_states, mask_index, cotangent, out_weight):

    def step(total, record):
        query_rec, key_rec, value_rec, mask_rec, cot_rec = record
        query_grad, key_grad, value_grad, weight_term = one_record(query_rec, key_rec, value_rec, mask_rec, cot_rec, out_weight)
        return (total + weight_term, (query_grad, key_grad, value_grad))
    start_total = jnp.zeros((HEADS * HEAD_DIM, D), jnp.float32)
    weight_grad, grads = lax.scan(step, start_total, (query_states, key_states, value_states, mask_index, cotangent))
    return (grads[0], grads[1], grads[2], weight_grad)
```

```python
import functools
import math

import jax
import jax.numpy as jnp
from jax import lax
from jax.experimental import pallas as pl
from jax.experimental.pallas import tpu as pltpu
from jax.sharding import PartitionSpec as P

HEAD_DIM = 128
SCALE = 1.0 / math.sqrt(HEAD_DIM)
BF = jnp.bfloat16
F32 = jnp.float32
ORDER = [(dz, dy) for dz in range(4) for dy in range(2)]
TOK = 128
MSK = 64
HEADS_DEV = 3


def move_blk(a, dz, dy):
    pairs = [
        (z * 2 + y, ((z + dz) % 4) * 2 + (y + dy) % 2) for z in range(4) for y in range(2)
    ]
    return lax.ppermute(a, "blk", pairs)


def move_dp(a, dx, dl, dc):
    pairs = [
        (x * 4 + l * 2 + c, ((x + dx) % 4) * 4 + ((l + dl) % 2) * 2 + (c + dc) % 2)
        for x in range(4)
        for l in range(2)
        for c in range(2)
    ]
    return lax.ppermute(a, "dp", pairs)


def dot(a, b, ca, cb):
    return lax.dot_general(a, b, (((ca,), (cb,)), ((), ())), preferred_element_type=F32)


def gather_y_first(c):
    half = c.shape[0]
    pair = jnp.concatenate([c, move_blk(c, 0, 1)], axis=0)
    one = move_blk(pair, 1, 0)
    three = move_blk(pair, 3, 0)
    two_a = move_blk(one[:half], 1, 0)
    two_b = move_blk(three[half:], 3, 0)
    return jnp.concatenate([pair, one, two_a, two_b, three], axis=0)


def gather_z_first(c):
    rows = c.shape[0]
    one = move_blk(c, 1, 0)
    three = move_blk(c, 3, 0)
    two = jnp.concatenate(
        [move_blk(one[: rows // 2], 1, 0), move_blk(three[rows // 2 :], 3, 0)], axis=0
    )
    mine = [c, one, two, three]
    other = move_blk(jnp.concatenate(mine, axis=0), 0, 1)
    parts = []
    for dz in range(4):
        parts += [mine[dz], other[dz * rows : (dz + 1) * rows]]
    return jnp.concatenate(parts, axis=0)


def forward_kernel(*refs):
    blocks, (prob_ref, att_ref) = refs[:8], refs[8:]
    query = jnp.concatenate([b[0:MSK] for b in blocks], axis=0)
    key = jnp.concatenate([b[MSK : MSK + TOK] for b in blocks], axis=0)
    value = jnp.concatenate([b[MSK + TOK :] for b in blocks], axis=0)
    scores = dot(key, query, 1, 1) * SCALE
    top = jnp.max(scores, axis=0, keepdims=True)
    raised = jnp.exp(scores - top)
    total = jnp.sum(raised, axis=0, keepdims=True)
    probs = (raised * (1.0 / total)).astype(BF)
    prob_ref[0] = probs
    att_ref[...] = dot(value.T, probs, 1, 0).astype(BF)


def backward_kernel(*refs):
    blocks, (prob_ref, att_ref, grad_ref), outs = refs[:8], refs[8:11], refs[11:]
    query = jnp.concatenate([b[0:MSK] for b in blocks], axis=0)
    key = jnp.concatenate([b[MSK : MSK + TOK] for b in blocks], axis=0)
    value = jnp.concatenate([b[MSK + TOK :] for b in blocks], axis=0)
    grad = grad_ref[...]
    delta = jnp.sum(grad.T.astype(F32) * att_ref[...].astype(F32), axis=0, keepdims=True)
    probs = prob_ref[0]
    prob_grad = dot(value, grad, 1, 1)
    score_grad = (probs.astype(F32) * (prob_grad - delta)).astype(BF)
    query_grad = (dot(key.T, score_grad, 1, 0) * SCALE).T.astype(BF)
    key_grad = (dot(score_grad, query, 1, 0) * SCALE).astype(BF)
    value_grad = dot(probs, grad, 1, 0).astype(BF)
    head = pl.program_id(0)

    def store(refs_, ids):
        for i in ids:
            refs_[i][0:MSK] = query_grad[i * MSK : (i + 1) * MSK]
            refs_[i][MSK : MSK + TOK] = key_grad[i * TOK : (i + 1) * TOK]
            refs_[i][MSK + TOK :] = value_grad[i * TOK : (i + 1) * TOK]

    store(outs, [i for i, (_, dy) in enumerate(ORDER) if dy == 0])

    @pl.when(head < 2)
    def _():
        store(outs, [i for i, (_, dy) in enumerate(ORDER) if dy == 1])


ROWS = MSK + 2 * TOK
QUERIES = 8 * MSK
KEYS = 8 * TOK


def forward(blocks):
    return pl.pallas_call(
        forward_kernel,
        grid=(HEADS_DEV,),
        in_specs=[pl.BlockSpec((ROWS, HEAD_DIM), lambda h: (0, h))] * 8,
        out_specs=[
            pl.BlockSpec((1, KEYS, QUERIES), lambda h: (h, 0, 0)),
            pl.BlockSpec((HEAD_DIM, QUERIES), lambda h: (h, 0)),
        ],
        out_shape=[
            jax.ShapeDtypeStruct((HEADS_DEV, KEYS, QUERIES), BF),
            jax.ShapeDtypeStruct((HEADS_DEV * HEAD_DIM, QUERIES), BF),
        ],
        compiler_params=pltpu.CompilerParams(vmem_limit_bytes=40 * 2**20),
        cost_estimate=pl.CostEstimate(
            flops=int(1.2e9), bytes_accessed=int(6e6), transcendentals=int(1.6e6)
        ),
    )(*blocks)


def backward(blocks, probs, att, grad):
    wide = lambda h: (0, h)
    narrow = lambda h: (0, jnp.minimum(h, 1))
    return pl.pallas_call(
        backward_kernel,
        grid=(HEADS_DEV,),
        in_specs=[pl.BlockSpec((ROWS, HEAD_DIM), wide)] * 8
        + [
            pl.BlockSpec((1, KEYS, QUERIES), lambda h: (h, 0, 0)),
            pl.BlockSpec((HEAD_DIM, QUERIES), lambda h: (h, 0)),
            pl.BlockSpec((QUERIES, HEAD_DIM), wide),
        ],
        out_specs=[
            pl.BlockSpec((ROWS, HEAD_DIM), narrow if dy else wide) for _, dy in ORDER
        ],
        out_shape=[
            jax.ShapeDtypeStruct((ROWS, HEAD_DIM * (2 if dy else 3)), BF) for _, dy in ORDER
        ],
        compiler_params=pltpu.CompilerParams(vmem_limit_bytes=40 * 2**20),
        cost_estimate=pl.CostEstimate(
            flops=int(3e9), bytes_accessed=int(9e6), transcendentals=0
        ),
    )(*blocks, probs, att, grad)


def shards(query_states, key_states, value_states, mask_index, cotangent, out_weight):
    blk, dp = lax.axis_index("blk"), lax.axis_index("dp")
    z, y = blk // 2, blk % 2
    x, lo, core = dp // 4, (dp // 2) % 2, dp % 2
    steps = mask_index[0] - blk * TOK
    selector = (steps[:, None] == jnp.arange(TOK, dtype=jnp.int32)[None, :]).astype(BF)
    masked_query = dot(selector, query_states[0], 1, 0).astype(BF)
    local = jnp.concatenate([masked_query, key_states[0], value_states[0]], axis=0)

    def slab(a, axis, zz, yy):
        own = lax.dynamic_slice_in_dim(a, zz * 640 + yy * 384, 256, axis)
        shared = lax.dynamic_slice_in_dim(a, zz * 640 + 256, 128, axis)
        return jnp.concatenate([own, shared], axis=axis)

    blocks = []
    for dz, dy in ORDER:
        piece = slab(local, 1, (z + dz) % 4, (y + dy) % 2)
        blocks.append(piece if (dz, dy) == (0, 0) else move_blk(piece, dz, dy))

    cot = cotangent[0]
    half = cot.shape[1] // 2
    cots = [gather_y_first(cot[:, :half]), gather_z_first(cot[:, half:])]
    weight = slab(out_weight, 0, z, y)

    probs, att = forward(blocks)
    grad = sum(dot(c, w, 1, 1) for c, w in zip(cots, (weight[:, :half], weight[:, half:])))
    outs = backward(blocks, probs, att, grad.astype(BF))

    r = jnp.arange(320, dtype=jnp.int32)
    rc, rx, rl, rr = r // 160, (r // 40) % 4, (r // 20) % 2, r % 20
    place = ((x + rx) % 4) * 80 + ((lo + rl) % 2) * 40 + ((core + rc) % 2) * 20 + rr
    wanted = place + y * 320
    index = jnp.where(
        (wanted >= 256) & (wanted < 384), wanted, jnp.where(y == 0, wanted, wanted - 384)
    )
    pick = (index[:, None] == jnp.arange(384, dtype=jnp.int32)[None, :]).astype(BF)
    att_rows = dot(pick, att, 1, 0).astype(BF)
    finals = []
    for c in cots:
        sent = move_dp(dot(att_rows[160:], c, 1, 0).astype(BF), 0, 0, 1)
        total = (dot(att_rows[:160], c, 1, 0) + sent.astype(F32)).astype(BF)
        chunks = [total[i * 40 : (i + 1) * 40] for i in range(4)]
        acc = chunks[0].astype(F32)
        for dx in (1, 2, 3):
            acc = acc + move_dp(chunks[dx], dx, 0, 0).astype(F32)
        finals.append(acc[:20] + move_dp(acc[20:].astype(BF), 0, 1, 0).astype(F32))
    weight_grad = jnp.concatenate(finals, axis=1)

    back = {}
    for (dz, dy), o in zip(ORDER, outs):
        back[(-dz) % 4, dy] = o if (dz, dy) == (0, 0) else move_blk(o, (-dz) % 4, dy)
    groups = []
    for dz in range(4):
        mine, other = back[(-dz) % 4, 0], back[(-dz) % 4, 1]
        groups.append(
            jnp.where(
                y == 0,
                jnp.concatenate([mine, other], axis=1),
                jnp.concatenate([other, mine[:, 256:], mine[:, :256]], axis=1),
            )
        )
    ring = jnp.concatenate(groups + groups[:3], axis=1)
    local_grad = lax.dynamic_slice_in_dim(ring, ((4 - z) % 4) * 640, 2560, 1)
    query_grad = dot(selector, local_grad[:MSK], 0, 0).astype(BF)
    return (
        query_grad[None],
        local_grad[None, MSK : MSK + TOK],
        local_grad[None, MSK + TOK :],
        weight_grad,
    )


def solution(mesh):
    return jax.shard_map(
        shards,
        mesh=mesh,
        in_specs=(
            P("dp", "blk", None),
            P("dp", "blk", None),
            P("dp", "blk", None),
            P("dp", "blk"),
            P("dp", "blk", None),
            P(),
        ),
        out_specs=(
            P("dp", "blk", None),
            P("dp", "blk", None),
            P("dp", "blk", None),
            P(("blk", "dp"), None),
        ),
        check_vma=False,
    )
```

```python
import math

import jax
import jax.numpy as jnp
from jax import lax
from jax.experimental import pallas as pl
from jax.experimental.pallas import tpu as pltpu
from jax.sharding import PartitionSpec as P

HEAD_DIM = 128
SCALE = 1.0 / math.sqrt(HEAD_DIM)
BF = jnp.bfloat16
F32 = jnp.float32
TOK = 128
MSK = 64
WIDTH = 2560
HEADS_DEV = 3
SLAB = HEADS_DEV * HEAD_DIM
QUERIES = 8 * MSK
KEYS = 8 * TOK
ROWS_OUT = MSK + 2 * TOK
ROWS_BACK = ROWS_OUT + 80
ROWS_IN = 2 * MSK + 2 * TOK
PARAMS = pltpu.CompilerParams(vmem_limit_bytes=40 * 2**20)


def exchange(a):
    return lax.all_to_all(a, "blk", 0, 0, tiled=True)


def move_x(a, dx):
    return lax.ppermute(a, "dp", [(i, (i + 4 * dx) % 16) for i in range(16)])


def move_y(a, dl, dh):
    pairs = []
    for i in range(128):
        b, d = i // 16, i % 16
        pairs.append((i, (b ^ dh) * 16 + (d ^ (2 * dl))))
    return lax.ppermute(a, ("blk", "dp"), pairs)


def move_z(a, dz):
    return lax.ppermute(a, "blk", [(i, (i + 2 * dz) % 8) for i in range(8)])


def swap_y(a):
    return lax.ppermute(a, "blk", [(i, i ^ 1) for i in range(8)])


def swap_core(a):
    return lax.ppermute(a, "dp", [(i, i ^ 1) for i in range(16)])


def dot(a, b, ca, cb):
    return lax.dot_general(a, b, (((ca,), (cb,)), ((), ())), preferred_element_type=F32)


def cost(flops, moved, exps=0):
    return pl.CostEstimate(flops=int(flops), bytes_accessed=int(moved), transcendentals=int(exps))


def slabs_of(query, grad, key, value):
    def kernel(*refs):
        out_ref = refs[4]
        for j in range(8):
            pair = (j // 2) * 640 + (j % 2) * 384
            shared = (j // 2) * 640 + 256
            row = 0
            for ref in refs[:4]:
                at = pl.ds(row, ref.shape[0])
                out_ref[j, at, 0:256] = ref[:, pair : pair + 256]
                out_ref[j, at, 256:SLAB] = ref[:, shared : shared + HEAD_DIM]
                row += ref.shape[0]

    return pl.pallas_call(
        kernel,
        out_shape=jax.ShapeDtypeStruct((8, ROWS_IN, SLAB), BF),
        compiler_params=PARAMS,
        cost_estimate=cost(0, ROWS_IN * WIDTH * 4.4),
    )(query, grad, key, value)


def outer(columns, att_rows, cot_parts):
    width = cot_parts[0].shape[1]
    rows = att_rows.shape[0] // 2
    tile = 512

    def kernel(column_ref, att_ref, *refs):
        att = jnp.concatenate(
            [
                att_ref[:, pl.ds(pl.multiple_of(column_ref[i], 2 * MSK), 2 * MSK)]
                for i in range(4)
            ],
            axis=1,
        )
        cots = jnp.concatenate([r[...] for r in refs[:4]], axis=0)
        refs[4][...] = dot(att[:rows], cots, 1, 0)
        refs[5][...] = dot(att[rows:], cots, 1, 0).astype(BF)

    out = pl.BlockSpec((rows, tile), lambda i, *_: (0, i))
    return pl.pallas_call(
        kernel,
        grid_spec=pltpu.PrefetchScalarGridSpec(
            num_scalar_prefetch=1,
            grid=(width // tile,),
            in_specs=[pl.BlockSpec((2 * rows, QUERIES), lambda i, *_: (0, 0))]
            + [pl.BlockSpec((2 * MSK, tile), lambda i, *_: (0, i))] * 4,
            out_specs=[out, out],
        ),
        out_shape=[
            jax.ShapeDtypeStruct((rows, width), F32),
            jax.ShapeDtypeStruct((rows, width), BF),
        ],
        compiler_params=PARAMS,
        cost_estimate=cost(1.4e9, 8e6),
    )(columns, att_rows, *cot_parts)


def finish(back, selector):
    def kernel(back_ref, selector_ref, query_ref, key_ref, value_ref):
        def put(to, query, key, value):
            query_ref[:, to] = dot(selector_ref[...], query, 0, 0).astype(BF)
            key_ref[:, to] = key
            value_ref[:, to] = value

        for j in range(8):
            at = (j // 2) * 640 + (j % 2) * 384
            put(
                slice(at, at + 256),
                back_ref[j, 0:MSK],
                back_ref[j, MSK : MSK + TOK],
                back_ref[j, MSK + TOK : ROWS_OUT],
            )
        for j in range(0, 8, 2):
            at = (j // 2) * 640 + 256
            halves = [
                jnp.concatenate(
                    [back_ref[k, ROWS_OUT:, 0:HEAD_DIM], back_ref[k, ROWS_OUT:, HEAD_DIM:]], axis=0
                )
                for k in (j, j + 1)
            ]
            query = jnp.concatenate([h[TOK:] for h in halves], axis=0)
            put(slice(at, at + HEAD_DIM), query, halves[0][0:TOK], halves[1][0:TOK])

    return pl.pallas_call(
        kernel,
        out_shape=[jax.ShapeDtypeStruct((TOK, WIDTH), BF)] * 3,
        compiler_params=PARAMS,
        cost_estimate=cost(5e7, 4e6),
    )(back, selector)


def forward_kernel(in_ref, prob_ref, att_ref):
    key = in_ref[:, 2 * MSK : 2 * MSK + TOK].reshape(KEYS, HEAD_DIM)
    value = in_ref[:, 2 * MSK + TOK :].reshape(KEYS, HEAD_DIM)
    query = in_ref[:, 0:MSK].reshape(QUERIES, HEAD_DIM)
    scores = dot(key, query, 1, 1) * SCALE
    top = jnp.max(scores, axis=0, keepdims=True)
    raised = jnp.exp(scores - top)
    total = jnp.sum(raised, axis=0, keepdims=True)
    probs = (raised * (1.0 / total)).astype(BF)
    prob_ref[0] = probs
    att_ref[...] = dot(value.T, probs, 1, 0).astype(BF)


def backward_kernel(place_ref, in_ref, prob_ref, att_ref, out_ref):
    key = in_ref[:, 2 * MSK : 2 * MSK + TOK].reshape(KEYS, HEAD_DIM)
    value = in_ref[:, 2 * MSK + TOK :].reshape(KEYS, HEAD_DIM)
    query = in_ref[:, 0:MSK].reshape(QUERIES, HEAD_DIM)
    grad = in_ref[:, MSK : 2 * MSK].reshape(QUERIES, HEAD_DIM)
    delta = jnp.sum(grad.T.astype(F32) * att_ref[...].astype(F32), axis=0, keepdims=True)
    probs = prob_ref[0]
    prob_grad = dot(value, grad, 1, 1)
    score_grad = (probs.astype(F32) * (prob_grad - delta)).astype(BF)
    query_grad = (dot(key.T, score_grad, 1, 0) * SCALE).T.astype(BF)
    key_grad = (dot(score_grad, query, 1, 0) * SCALE).astype(BF)
    value_grad = dot(probs, grad, 1, 0).astype(BF)
    head = pl.program_id(0)
    query_grad = query_grad.reshape(8, MSK, HEAD_DIM)
    key_grad = key_grad.reshape(8, TOK, HEAD_DIM)
    value_grad = value_grad.reshape(8, TOK, HEAD_DIM)

    def own(at):
        out_ref[:, 0:MSK, at] = query_grad
        out_ref[:, MSK : MSK + TOK, at] = key_grad
        out_ref[:, MSK + TOK : ROWS_OUT, at] = value_grad

    @pl.when(head == 0)
    def _():
        own(slice(0, HEAD_DIM))

    @pl.when(head == 1)
    def _():
        own(slice(HEAD_DIM, 2 * HEAD_DIM))

    def half(grad, query):
        out_ref[:, ROWS_OUT:, 0:HEAD_DIM] = grad[:, 0:80]
        out_ref[:, ROWS_OUT : ROWS_OUT + 48, HEAD_DIM:] = grad[:, 80:]
        out_ref[:, ROWS_OUT + 48 :, HEAD_DIM:] = query

    @pl.when((head == 2) & (place_ref[0] == 0))
    def _():
        half(key_grad, query_grad[:, 0:32])

    @pl.when((head == 2) & (place_ref[0] == 1))
    def _():
        half(value_grad, query_grad[:, 32:])


def head_block(rows):
    return pl.BlockSpec((8, rows, HEAD_DIM), lambda h, *_: (0, 0, h))


PROB_BLOCK = pl.BlockSpec((1, KEYS, QUERIES), lambda h, *_: (h, 0, 0))
ATT_BLOCK = pl.BlockSpec((HEAD_DIM, QUERIES), lambda h, *_: (h, 0))


def forward(sent):
    return pl.pallas_call(
        forward_kernel,
        grid=(HEADS_DEV,),
        in_specs=[head_block(ROWS_IN)],
        out_specs=[PROB_BLOCK, ATT_BLOCK],
        out_shape=[
            jax.ShapeDtypeStruct((HEADS_DEV, KEYS, QUERIES), BF),
            jax.ShapeDtypeStruct((SLAB, QUERIES), BF),
        ],
        compiler_params=PARAMS,
        cost_estimate=cost(1.2e9, 6e6, 1.6e6),
    )(sent)


def backward(place, sent, probs, att):
    return pl.pallas_call(
        backward_kernel,
        grid_spec=pltpu.PrefetchScalarGridSpec(
            num_scalar_prefetch=1,
            grid=(HEADS_DEV,),
            in_specs=[head_block(ROWS_IN), PROB_BLOCK, ATT_BLOCK],
            out_specs=pl.BlockSpec((8, ROWS_BACK, 2 * HEAD_DIM), lambda h, *_: (0, 0, 0)),
        ),
        out_shape=jax.ShapeDtypeStruct((8, ROWS_BACK, 2 * HEAD_DIM), BF),
        compiler_params=PARAMS,
        cost_estimate=cost(3e9, 9e6),
    )(place, sent, probs, att)


def shards(query_states, key_states, value_states, mask_index, cotangent, out_weight):
    blk, dp = lax.axis_index("blk"), lax.axis_index("dp")
    z, y, core = blk // 2, blk % 2, dp % 2
    x, low = dp // 4, (dp // 2) % 2
    steps = mask_index[0] - blk * TOK

    cot = cotangent[0]
    half = cot.shape[1] // 2
    cot_kept = lax.dynamic_slice_in_dim(cot, y * half, half, 1)
    cot_got = swap_y(lax.dynamic_slice_in_dim(cot, (1 - y) * half, half, 1))
    steps, cot_got = lax.optimization_barrier((steps, cot_got))
    cot_pair = jnp.where(
        y == 0,
        jnp.concatenate([cot_kept, cot_got], axis=0),
        jnp.concatenate([cot_got, cot_kept], axis=0),
    )

    selector = (steps[:, None] == jnp.arange(TOK, dtype=jnp.int32)[None, :]).astype(BF)
    masked_query = dot(selector, query_states[0], 1, 0).astype(BF)
    masked_grad = dot(cot, out_weight, 1, 1).astype(BF)
    heads_in = exchange(
        slabs_of(masked_query, masked_grad, key_states[0], value_states[0])
    )
    cot_parts = [cot_pair] + [move_z(cot_pair, dz) for dz in (3, 2, 1)]
    probs, att = forward(heads_in)
    att_got = swap_y(att[:256])
    outs = backward(y[None].astype(jnp.int32), heads_in, probs, att)

    back = exchange(outs)
    cot_parts, att_got, _ = lax.optimization_barrier((cot_parts, att_got, outs))
    r = jnp.arange(640, dtype=jnp.int32)
    rc, rx, rl, rh, rr = r // 320, (r // 80) % 4, (r // 40) % 2, (r // 20) % 2, r % 20
    wanted = (
        ((y + rh) % 2) * 320
        + ((x + rx) % 4) * 80
        + ((low + rl) % 2) * 40
        + ((core + rc) % 2) * 20
        + rr
    )
    low_place = jnp.where(y == 0, wanted, wanted + 384)
    high_place = jnp.where(y == 0, wanted, wanted - 384)
    index = jnp.where(wanted < 256, low_place, jnp.where(wanted < 384, wanted, high_place))
    pick = (index[:, None] == r[None, :]).astype(BF)
    att_rows = (dot(pick[:, :SLAB], att, 1, 0) + dot(pick[:, SLAB:], att_got, 1, 0)).astype(BF)
    columns = (z + jnp.arange(4, dtype=jnp.int32)) % 4 * (2 * MSK)
    kept, sent = outer(columns, att_rows, cot_parts)
    sent = swap_core(sent)
    chunks = [
        kept[i * 80 : (i + 1) * 80] + sent[i * 80 : (i + 1) * 80].astype(F32) for i in range(4)
    ]
    acc = chunks[0]
    for dx in (1, 2, 3):
        acc = acc + move_x(chunks[dx].astype(BF), dx).astype(F32)
    back, acc = lax.optimization_barrier((back, acc))
    quarter = acc.astype(BF)
    own_half = acc[:20] + move_y(quarter[40:60], 1, 0).astype(F32)
    other_half = move_y(quarter[20:40], 0, 1).astype(F32) + move_y(quarter[60:], 1, 1).astype(F32)
    weight_grad = jnp.where(
        y == 0,
        jnp.concatenate([own_half, other_half], axis=1),
        jnp.concatenate([other_half, own_half], axis=1),
    )

    grads = finish(back, selector)
    return (*(g[None] for g in grads), weight_grad)


def solution(mesh):
    return jax.shard_map(
        shards,
        mesh=mesh,
        in_specs=(
            P("dp", "blk", None),
            P("dp", "blk", None),
            P("dp", "blk", None),
            P("dp", "blk"),
            P("dp", "blk", None),
            P(),
        ),
        out_specs=(
            P("dp", "blk", None),
            P("dp", "blk", None),
            P("dp", "blk", None),
            P(("blk", "dp"), None),
        ),
        check_vma=False,
    )
```

```python
import math

import jax
import jax.numpy as jnp
from jax import lax
from jax.experimental import pallas as pl
from jax.experimental.pallas import tpu as pltpu
from jax.sharding import PartitionSpec as P

HEAD_DIM = 128
SCALE = 1.0 / math.sqrt(HEAD_DIM)
BF = jnp.bfloat16
F32 = jnp.float32
TOK = 128
MSK = 64
WIDTH = 2560
HEADS_DEV = 3
SLAB = HEADS_DEV * HEAD_DIM
QUERIES = 8 * MSK
KEYS = 8 * TOK
ROWS_OUT = MSK + 2 * TOK
ROWS_BACK = ROWS_OUT + 80
PARAMS = pltpu.CompilerParams(vmem_limit_bytes=40 * 2**20)


def exchange(a):
    return lax.all_to_all(a, "blk", 0, 0, tiled=True)


def move_x(a, dx):
    return lax.ppermute(a, "dp", [(i, (i + 4 * dx) % 16) for i in range(16)])


def move_y(a, dl, dh):
    pairs = []
    for i in range(128):
        b, d = i // 16, i % 16
        pairs.append((i, (b ^ dh) * 16 + (d ^ (2 * dl))))
    return lax.ppermute(a, ("blk", "dp"), pairs)


def move_z(a, dz):
    return lax.ppermute(a, "blk", [(i, (i + 2 * dz) % 8) for i in range(8)])


def swap_y(a):
    return lax.ppermute(a, "blk", [(i, i ^ 1) for i in range(8)])


def swap_core(a):
    return lax.ppermute(a, "dp", [(i, i ^ 1) for i in range(16)])


def dot(a, b, ca, cb):
    return lax.dot_general(a, b, (((ca,), (cb,)), ((), ())), preferred_element_type=F32)


def cost(flops, moved, exps=0):
    return pl.CostEstimate(flops=int(flops), bytes_accessed=int(moved), transcendentals=int(exps))


def slabs_of(query, key, value):
    def kernel(*refs):
        out_ref = refs[3]
        for j in range(8):
            pair = (j // 2) * 640 + (j % 2) * 384
            shared = (j // 2) * 640 + 256
            row = 0
            for ref in refs[:3]:
                at = pl.ds(row, ref.shape[0])
                out_ref[j, at, 0:256] = ref[:, pair : pair + 256]
                out_ref[j, at, 256:SLAB] = ref[:, shared : shared + HEAD_DIM]
                row += ref.shape[0]

    return pl.pallas_call(
        kernel,
        out_shape=jax.ShapeDtypeStruct((8, ROWS_OUT, SLAB), BF),
        compiler_params=PARAMS,
        cost_estimate=cost(0, ROWS_OUT * WIDTH * 4.4),
    )(query, key, value)


def pack_grads(starts, grad):
    def kernel(start_ref, grad_ref, *outs):
        for i, out_ref in enumerate(outs):
            out_ref[...] = grad_ref[:, pl.ds(pl.multiple_of(start_ref[i], HEAD_DIM), 640)]

    vmem = pl.BlockSpec(memory_space=pltpu.VMEM)
    return pl.pallas_call(
        kernel,
        in_specs=[pl.BlockSpec(memory_space=pltpu.SMEM), vmem],
        out_shape=[jax.ShapeDtypeStruct((MSK, 640), BF)] * 4,
        compiler_params=PARAMS,
        cost_estimate=cost(0, MSK * WIDTH * 4),
    )(starts, grad)


def outer(att_rows, cot_parts):
    width = cot_parts[0].shape[1]
    rows = att_rows.shape[0] // 2
    tile = 1024

    def kernel(att_ref, *refs):
        att = att_ref[...]
        cots = jnp.concatenate([r[...] for r in refs[:4]], axis=0)
        refs[4][...] = dot(att[:rows], cots, 1, 0).astype(BF)
        refs[5][...] = dot(att[rows:], cots, 1, 0).astype(BF)

    out = pl.BlockSpec((rows, tile), lambda i: (0, i))
    return pl.pallas_call(
        kernel,
        grid=(width // tile,),
        in_specs=[pl.BlockSpec((2 * rows, QUERIES), lambda i: (0, 0))]
        + [pl.BlockSpec((2 * MSK, tile), lambda i: (0, i))] * 4,
        out_specs=[out, out],
        out_shape=[
            jax.ShapeDtypeStruct((rows, width), BF),
            pltpu.HBM((rows, width), BF),
        ],
        compiler_params=PARAMS,
        cost_estimate=cost(1.4e9, 8e6),
    )(att_rows, *cot_parts)


def finish(back, selector):
    def kernel(back_ref, selector_ref, query_ref, key_ref, value_ref):
        def put(to, query, key, value):
            query_ref[:, to] = dot(selector_ref[...], query, 0, 0).astype(BF)
            key_ref[:, to] = key
            value_ref[:, to] = value

        for j in range(8):
            at = (j // 2) * 640 + (j % 2) * 384
            put(
                slice(at, at + 256),
                back_ref[j, 0:MSK],
                back_ref[j, MSK : MSK + TOK],
                back_ref[j, MSK + TOK : ROWS_OUT],
            )
        for j in range(0, 8, 2):
            at = (j // 2) * 640 + 256
            halves = [
                jnp.concatenate(
                    [back_ref[k, ROWS_OUT:, 0:HEAD_DIM], back_ref[k, ROWS_OUT:, HEAD_DIM:]], axis=0
                )
                for k in (j, j + 1)
            ]
            query = jnp.concatenate([h[TOK:] for h in halves], axis=0)
            put(slice(at, at + HEAD_DIM), query, halves[0][0:TOK], halves[1][0:TOK])

    return pl.pallas_call(
        kernel,
        out_shape=[jax.ShapeDtypeStruct((TOK, WIDTH), BF)] * 3,
        compiler_params=PARAMS,
        cost_estimate=cost(2e10, 4e6),
    )(back, selector)


def forward_kernel(in_ref, prob_ref, att_ref):
    key = in_ref[:, MSK : MSK + TOK].reshape(KEYS, HEAD_DIM)
    value = in_ref[:, MSK + TOK :].reshape(KEYS, HEAD_DIM)
    query = in_ref[:, 0:MSK].reshape(QUERIES, HEAD_DIM)
    scores = dot(key, query, 1, 1) * SCALE
    top = jnp.max(scores, axis=0, keepdims=True)
    raised = jnp.exp(scores - top)
    total = jnp.sum(raised, axis=0, keepdims=True)
    probs = (raised * (1.0 / total)).astype(BF)
    prob_ref[0] = probs
    att_ref[...] = dot(value.T, probs, 1, 0).astype(BF)


def backward_kernel(place_ref, in_ref, *refs):
    own_refs, (got_ref, prob_ref, att_ref, out_ref, grad_ref) = refs[:4], refs[4:]
    key = in_ref[:, MSK : MSK + TOK].reshape(KEYS, HEAD_DIM)
    value = in_ref[:, MSK + TOK :].reshape(KEYS, HEAD_DIM)
    query = in_ref[:, 0:MSK].reshape(QUERIES, HEAD_DIM)
    for i in range(4):
        mine = pl.multiple_of(place_ref[4 + i] + place_ref[0] * MSK, MSK)
        other = pl.multiple_of(place_ref[4 + i] + (1 - place_ref[0]) * MSK, MSK)
        grad_ref[pl.ds(mine, MSK)] = own_refs[i][...]
        grad_ref[pl.ds(other, MSK)] = got_ref[i * MSK : (i + 1) * MSK]
    grad = grad_ref[...]
    delta = jnp.sum(grad.T.astype(F32) * att_ref[...].astype(F32), axis=0, keepdims=True)
    probs = prob_ref[0]
    prob_grad = dot(value, grad, 1, 1)
    score_grad = (probs.astype(F32) * (prob_grad - delta)).astype(BF)
    query_grad = (dot(key.T, score_grad, 1, 0) * SCALE).T.astype(BF)
    key_grad = (dot(score_grad, query, 1, 0) * SCALE).astype(BF)
    value_grad = dot(probs, grad, 1, 0).astype(BF)
    head = pl.program_id(0)
    query_grad = query_grad.reshape(8, MSK, HEAD_DIM)
    key_grad = key_grad.reshape(8, TOK, HEAD_DIM)
    value_grad = value_grad.reshape(8, TOK, HEAD_DIM)

    def own(at):
        out_ref[:, 0:MSK, at] = query_grad
        out_ref[:, MSK : MSK + TOK, at] = key_grad
        out_ref[:, MSK + TOK : ROWS_OUT, at] = value_grad

    @pl.when(head == 0)
    def _():
        own(slice(0, HEAD_DIM))

    @pl.when(head == 1)
    def _():
        own(slice(HEAD_DIM, 2 * HEAD_DIM))

    def half(grad, query):
        out_ref[:, ROWS_OUT:, 0:HEAD_DIM] = grad[:, 0:80]
        out_ref[:, ROWS_OUT : ROWS_OUT + 48, HEAD_DIM:] = grad[:, 80:]
        out_ref[:, ROWS_OUT + 48 :, HEAD_DIM:] = query

    @pl.when((head == 2) & (place_ref[0] == 0))
    def _():
        half(key_grad, query_grad[:, 0:32])

    @pl.when((head == 2) & (place_ref[0] == 1))
    def _():
        half(value_grad, query_grad[:, 32:])


def head_block(rows):
    return pl.BlockSpec((8, rows, HEAD_DIM), lambda h, *_: (0, 0, h))


PROB_BLOCK = pl.BlockSpec((1, KEYS, QUERIES), lambda h, *_: (h, 0, 0))
ATT_BLOCK = pl.BlockSpec((HEAD_DIM, QUERIES), lambda h, *_: (h, 0))


def forward(sent):
    return pl.pallas_call(
        forward_kernel,
        grid=(HEADS_DEV,),
        in_specs=[head_block(ROWS_OUT)],
        out_specs=[PROB_BLOCK, ATT_BLOCK],
        out_shape=[
            jax.ShapeDtypeStruct((HEADS_DEV, KEYS, QUERIES), BF),
            jax.ShapeDtypeStruct((SLAB, QUERIES), BF),
        ],
        compiler_params=PARAMS,
        cost_estimate=cost(1e6, 1e5),
    )(sent)


def backward(place, sent, own, got, probs, att):
    return pl.pallas_call(
        backward_kernel,
        grid_spec=pltpu.PrefetchScalarGridSpec(
            num_scalar_prefetch=1,
            grid=(HEADS_DEV,),
            in_specs=[
                head_block(ROWS_OUT),
                *[pl.BlockSpec((MSK, HEAD_DIM), lambda h, place: (0, place[1 + h]))] * 4,
                pl.BlockSpec((4 * MSK, HEAD_DIM), lambda h, *_: (0, h)),
                PROB_BLOCK,
                ATT_BLOCK,
            ],
            out_specs=pl.BlockSpec((8, ROWS_BACK, 2 * HEAD_DIM), lambda h, *_: (0, 0, 0)),
            scratch_shapes=[pltpu.VMEM((QUERIES, HEAD_DIM), BF)],
        ),
        out_shape=jax.ShapeDtypeStruct((8, ROWS_BACK, 2 * HEAD_DIM), BF),
        compiler_params=PARAMS,
        cost_estimate=cost(1e6, 1e5),
    )(place, sent, *own, got, probs, att)


def shards(query_states, key_states, value_states, mask_index, cotangent, out_weight):
    blk, dp = lax.axis_index("blk"), lax.axis_index("dp")
    z, y, core = blk // 2, blk % 2, dp % 2
    x, low = dp // 4, (dp // 2) % 2
    steps = mask_index[0] - blk * TOK

    cot = cotangent[0]
    half = cot.shape[1] // 2
    cot_kept = lax.dynamic_slice_in_dim(cot, y * half, half, 1)
    cot_got = swap_y(lax.dynamic_slice_in_dim(cot, (1 - y) * half, half, 1))
    cot_pair = jnp.where(
        y == 0,
        jnp.concatenate([cot_kept, cot_got], axis=0),
        jnp.concatenate([cot_got, cot_kept], axis=0),
    )

    selector = (steps[:, None] == jnp.arange(TOK, dtype=jnp.int32)[None, :]).astype(BF)
    masked_query = dot(selector, query_states[0], 1, 0).astype(BF)
    packed = slabs_of(masked_query, key_states[0], value_states[0])
    heads_in = exchange(packed)
    masked_grad = dot(cot, out_weight, 1, 1).astype(BF)
    ring = (z + jnp.arange(4, dtype=jnp.int32)) % 4
    columns = ring * (2 * MSK)
    grads_out = pack_grads(ring * 640, masked_grad)
    own_grad = [grads_out[0]] + [move_z(grads_out[4 - dz], 4 - dz) for dz in (1, 2, 3)]
    own_all = jnp.concatenate(own_grad, axis=0)
    got_grad = swap_y(
        jnp.concatenate(
            [lax.dynamic_slice_in_dim(own_all, (1 - y) * 384, 256, 1), own_all[:, 256:384]], axis=1
        )
    )
    place = jnp.concatenate([jnp.stack([y, 3 * y, 3 * y + 1, 0 * y + 2]), columns]).astype(jnp.int32)
    cot_parts = [cot_pair] + [move_z(cot_pair, dz) for dz in (3, 2, 1)]
    probs, att = forward(heads_in)
    att_got = swap_y(att[:256])
    outs = backward(place, heads_in, own_grad, got_grad, probs, att)

    back = exchange(outs)
    cot_parts, att_got, _ = lax.optimization_barrier((cot_parts, att_got, outs))
    r = jnp.arange(640, dtype=jnp.int32)
    rc, rx, rl, rh, rr = r // 320, (r // 80) % 4, (r // 40) % 2, (r // 20) % 2, r % 20
    wanted = (
        ((y + rh) % 2) * 320
        + ((x + rx) % 4) * 80
        + ((low + rl) % 2) * 40
        + ((core + rc) % 2) * 20
        + rr
    )
    low_place = jnp.where(y == 0, wanted, wanted + 384)
    high_place = jnp.where(y == 0, wanted, wanted - 384)
    index = jnp.where(wanted < 256, low_place, jnp.where(wanted < 384, wanted, high_place))
    pick = (index[:, None] == r[None, :]).astype(BF)
    att_rows = (dot(pick[:, :SLAB], att, 1, 0) + dot(pick[:, SLAB:], att_got, 1, 0)).astype(BF)
    att_rows = lax.dynamic_slice_in_dim(
        jnp.concatenate([att_rows, att_rows], axis=1), z * 2 * MSK, QUERIES, 1
    )
    kept, sent = outer(att_rows, cot_parts)
    sent = swap_core(sent)
    chunks = [
        kept[i * 80 : (i + 1) * 80].astype(F32) + sent[i * 80 : (i + 1) * 80].astype(F32) for i in range(4)
    ]
    acc = chunks[0]
    for dx in (1, 2, 3):
        acc = acc + move_x(chunks[dx].astype(BF), dx).astype(F32)
    back, _ = lax.optimization_barrier((back, acc))
    quarter = acc.astype(BF)
    own_half = acc[:20] + move_y(quarter[40:60], 1, 0).astype(F32)
    other_half = move_y(quarter[20:40], 0, 1).astype(F32) + move_y(quarter[60:], 1, 1).astype(F32)
    weight_grad = jnp.where(
        y == 0,
        jnp.concatenate([own_half, other_half], axis=1),
        jnp.concatenate([other_half, own_half], axis=1),
    )

    grads = finish(back, selector)
    return (*(g[None] for g in grads), weight_grad)


def solution(mesh):
    return jax.shard_map(
        shards,
        mesh=mesh,
        in_specs=(
            P("dp", "blk", None),
            P("dp", "blk", None),
            P("dp", "blk", None),
            P("dp", "blk"),
            P("dp", "blk", None),
            P(),
        ),
        out_specs=(
            P("dp", "blk", None),
            P("dp", "blk", None),
            P("dp", "blk", None),
            P(("blk", "dp"), None),
        ),
        check_vma=False,
    )
```

```python
import math

import jax
import jax.numpy as jnp
from jax import lax
from jax.experimental import pallas as pl
from jax.experimental.pallas import tpu as pltpu
from jax.sharding import PartitionSpec as P

HEAD_DIM = 128
SCALE = 1.0 / math.sqrt(HEAD_DIM)
BF = jnp.bfloat16
F32 = jnp.float32
TOK = 128
MSK = 64
WIDTH = 2560
HEADS_DEV = 3
SLAB = HEADS_DEV * HEAD_DIM
QUERIES = 8 * MSK
KEYS = 8 * TOK
ROWS_OUT = MSK + 2 * TOK
ROWS_BACK = ROWS_OUT + 80
PARAMS = pltpu.CompilerParams(vmem_limit_bytes=40 * 2**20)


def exchange(a):
    return lax.all_to_all(a, "blk", 0, 0, tiled=True)


def move_x(a, dx):
    return lax.ppermute(a, "dp", [(i, (i + 4 * dx) % 16) for i in range(16)])


def move_y(a, dl, dh):
    pairs = []
    for i in range(128):
        b, d = i // 16, i % 16
        pairs.append((i, (b ^ dh) * 16 + (d ^ (2 * dl))))
    return lax.ppermute(a, ("blk", "dp"), pairs)


def move_z(a, dz):
    return lax.ppermute(a, "blk", [(i, (i + 2 * dz) % 8) for i in range(8)])


def swap_y(a):
    return lax.ppermute(a, "blk", [(i, i ^ 1) for i in range(8)])


def swap_core(a):
    return lax.ppermute(a, "dp", [(i, i ^ 1) for i in range(16)])


def dot(a, b, ca, cb):
    return lax.dot_general(a, b, (((ca,), (cb,)), ((), ())), preferred_element_type=F32)


def cost(flops, moved, exps=0):
    return pl.CostEstimate(flops=int(flops), bytes_accessed=int(moved), transcendentals=int(exps))


def slabs_of(query, key, value):
    def kernel(*refs):
        out_ref = refs[3]
        for j in range(8):
            pair = (j // 2) * 640 + (j % 2) * 384
            shared = (j // 2) * 640 + 256
            row = 0
            for ref in refs[:3]:
                at = pl.ds(row, ref.shape[0])
                out_ref[j, at, 0:256] = ref[:, pair : pair + 256]
                out_ref[j, at, 256:SLAB] = ref[:, shared : shared + HEAD_DIM]
                row += ref.shape[0]

    return pl.pallas_call(
        kernel,
        out_shape=jax.ShapeDtypeStruct((8, ROWS_OUT, SLAB), BF),
        compiler_params=PARAMS,
        cost_estimate=cost(0, ROWS_OUT * WIDTH * 4.4),
    )(query, key, value)


def pack_grads(starts, grad):
    def kernel(start_ref, grad_ref, *outs):
        for i, out_ref in enumerate(outs):
            out_ref[...] = grad_ref[:, pl.ds(pl.multiple_of(start_ref[i], HEAD_DIM), 640)]

    vmem = pl.BlockSpec(memory_space=pltpu.VMEM)
    return pl.pallas_call(
        kernel,
        in_specs=[pl.BlockSpec(memory_space=pltpu.SMEM), vmem],
        out_shape=[jax.ShapeDtypeStruct((MSK, 640), BF)] * 4,
        compiler_params=PARAMS,
        cost_estimate=cost(0, MSK * WIDTH * 4),
    )(starts, grad)


def outer(place, att_rows, own_parts, other_parts):
    width = other_parts[0].shape[1]
    rows = att_rows.shape[0] // 2
    tile = 1024

    def kernel(place_ref, att_ref, *refs):
        first = place_ref[0] == 0
        blocks = []
        for own, other in zip(refs[:4], refs[4:8]):
            blocks.append(jnp.where(first, own[...], other[...]))
            blocks.append(jnp.where(first, other[...], own[...]))
        cots = jnp.concatenate(blocks, axis=0)
        refs[8][...] = dot(att_ref[:rows], cots, 1, 0).astype(BF)
        refs[9][...] = dot(att_ref[rows:], cots, 1, 0).astype(BF)

    out = pl.BlockSpec((rows, tile), lambda i, *_: (0, i))
    return pl.pallas_call(
        kernel,
        grid_spec=pltpu.PrefetchScalarGridSpec(
            num_scalar_prefetch=1,
            grid=(width // tile,),
            in_specs=[pl.BlockSpec((2 * rows, QUERIES), lambda i, *_: (0, 0))]
            + [pl.BlockSpec((MSK, tile), lambda i, *_: (0, i))] * 8,
            out_specs=[out, out],
        ),
        out_shape=[
            pltpu.HBM((rows, width), BF),
            pltpu.HBM((rows, width), BF),
        ],
        compiler_params=PARAMS,
        cost_estimate=cost(1.4e9, 8e6),
    )(place, att_rows, *own_parts, *other_parts)


def finish(back, selector):
    def kernel(back_ref, selector_ref, query_ref, key_ref, value_ref):
        def put(to, query, key, value):
            query_ref[:, to] = dot(selector_ref[...], query, 0, 0).astype(BF)
            key_ref[:, to] = key
            value_ref[:, to] = value

        for j in range(8):
            at = (j // 2) * 640 + (j % 2) * 384
            put(
                slice(at, at + 256),
                back_ref[j, 0:MSK],
                back_ref[j, MSK : MSK + TOK],
                back_ref[j, MSK + TOK : ROWS_OUT],
            )
        for j in range(0, 8, 2):
            at = (j // 2) * 640 + 256
            halves = [
                jnp.concatenate(
                    [back_ref[k, ROWS_OUT:, 0:HEAD_DIM], back_ref[k, ROWS_OUT:, HEAD_DIM:]], axis=0
                )
                for k in (j, j + 1)
            ]
            query = jnp.concatenate([h[TOK:] for h in halves], axis=0)
            put(slice(at, at + HEAD_DIM), query, halves[0][0:TOK], halves[1][0:TOK])

    return pl.pallas_call(
        kernel,
        out_shape=[jax.ShapeDtypeStruct((TOK, WIDTH), BF)] * 3,
        compiler_params=PARAMS,
        cost_estimate=cost(2e10, 4e6),
    )(back, selector)


def forward_kernel(in_ref, prob_ref, att_ref):
    key = in_ref[:, MSK : MSK + TOK].reshape(KEYS, HEAD_DIM)
    value = in_ref[:, MSK + TOK :].reshape(KEYS, HEAD_DIM)
    query = in_ref[:, 0:MSK].reshape(QUERIES, HEAD_DIM)
    scores = dot(key, query, 1, 1) * SCALE
    top = jnp.max(scores, axis=0, keepdims=True)
    raised = jnp.exp(scores - top)
    total = jnp.sum(raised, axis=0, keepdims=True)
    probs = (raised * (1.0 / total)).astype(BF)
    prob_ref[0] = probs
    att_ref[...] = dot(value.T, probs, 1, 0).astype(BF)


def backward_kernel(place_ref, in_ref, *refs):
    own_refs, (got_ref, prob_ref, att_ref, out_ref, grad_ref) = refs[:4], refs[4:]
    key = in_ref[:, MSK : MSK + TOK].reshape(KEYS, HEAD_DIM)
    value = in_ref[:, MSK + TOK :].reshape(KEYS, HEAD_DIM)
    query = in_ref[:, 0:MSK].reshape(QUERIES, HEAD_DIM)
    for i in range(4):
        mine = pl.multiple_of(place_ref[4 + i] + place_ref[0] * MSK, MSK)
        other = pl.multiple_of(place_ref[4 + i] + (1 - place_ref[0]) * MSK, MSK)
        grad_ref[pl.ds(mine, MSK)] = own_refs[i][...]
        grad_ref[pl.ds(other, MSK)] = got_ref[i * MSK : (i + 1) * MSK]
    grad = grad_ref[...]
    delta = jnp.sum(grad.T.astype(F32) * att_ref[...].astype(F32), axis=0, keepdims=True)
    probs = prob_ref[0]
    prob_grad = dot(value, grad, 1, 1)
    score_grad = (probs.astype(F32) * (prob_grad - delta)).astype(BF)
    query_grad = (dot(key.T, score_grad, 1, 0) * SCALE).T.astype(BF)
    key_grad = (dot(score_grad, query, 1, 0) * SCALE).astype(BF)
    value_grad = dot(probs, grad, 1, 0).astype(BF)
    head = pl.program_id(0)
    query_grad = query_grad.reshape(8, MSK, HEAD_DIM)
    key_grad = key_grad.reshape(8, TOK, HEAD_DIM)
    value_grad = value_grad.reshape(8, TOK, HEAD_DIM)

    def own(at):
        out_ref[:, 0:MSK, at] = query_grad
        out_ref[:, MSK : MSK + TOK, at] = key_grad
        out_ref[:, MSK + TOK : ROWS_OUT, at] = value_grad

    @pl.when(head == 0)
    def _():
        own(slice(0, HEAD_DIM))

    @pl.when(head == 1)
    def _():
        own(slice(HEAD_DIM, 2 * HEAD_DIM))

    def half(grad, query):
        out_ref[:, ROWS_OUT:, 0:HEAD_DIM] = grad[:, 0:80]
        out_ref[:, ROWS_OUT : ROWS_OUT + 48, HEAD_DIM:] = grad[:, 80:]
        out_ref[:, ROWS_OUT + 48 :, HEAD_DIM:] = query

    @pl.when((head == 2) & (place_ref[0] == 0))
    def _():
        half(key_grad, query_grad[:, 0:32])

    @pl.when((head == 2) & (place_ref[0] == 1))
    def _():
        half(value_grad, query_grad[:, 32:])


def head_block(rows):
    return pl.BlockSpec((8, rows, HEAD_DIM), lambda h, *_: (0, 0, h))


PROB_BLOCK = pl.BlockSpec((1, KEYS, QUERIES), lambda h, *_: (h, 0, 0))
ATT_BLOCK = pl.BlockSpec((HEAD_DIM, QUERIES), lambda h, *_: (h, 0))


def forward(sent):
    return pl.pallas_call(
        forward_kernel,
        grid=(HEADS_DEV,),
        in_specs=[head_block(ROWS_OUT)],
        out_specs=[PROB_BLOCK, ATT_BLOCK],
        out_shape=[
            jax.ShapeDtypeStruct((HEADS_DEV, KEYS, QUERIES), BF),
            jax.ShapeDtypeStruct((SLAB, QUERIES), BF),
        ],
        compiler_params=PARAMS,
        cost_estimate=cost(1e6, 1e5),
    )(sent)


def backward(place, sent, own, got, probs, att):
    return pl.pallas_call(
        backward_kernel,
        grid_spec=pltpu.PrefetchScalarGridSpec(
            num_scalar_prefetch=1,
            grid=(HEADS_DEV,),
            in_specs=[
                head_block(ROWS_OUT),
                *[pl.BlockSpec((MSK, HEAD_DIM), lambda h, place: (0, place[1 + h]))] * 4,
                pl.BlockSpec((4 * MSK, HEAD_DIM), lambda h, *_: (0, h)),
                PROB_BLOCK,
                ATT_BLOCK,
            ],
            out_specs=pl.BlockSpec((8, ROWS_BACK, 2 * HEAD_DIM), lambda h, *_: (0, 0, 0)),
            scratch_shapes=[pltpu.VMEM((QUERIES, HEAD_DIM), BF)],
        ),
        out_shape=pltpu.HBM((8, ROWS_BACK, 2 * HEAD_DIM), BF),
        compiler_params=PARAMS,
        cost_estimate=cost(1e6, 1e5),
    )(place, sent, *own, got, probs, att)


def shards(query_states, key_states, value_states, mask_index, cotangent, out_weight):
    blk, dp = lax.axis_index("blk"), lax.axis_index("dp")
    z, y, core = blk // 2, blk % 2, dp % 2
    x, low = dp // 4, (dp // 2) % 2
    steps = mask_index[0] - blk * TOK

    cot = cotangent[0]
    half = cot.shape[1] // 2
    cot_kept = lax.dynamic_slice_in_dim(cot, y * half, half, 1)
    cot_got = swap_y(lax.dynamic_slice_in_dim(cot, (1 - y) * half, half, 1))
    selector = (steps[:, None] == jnp.arange(TOK, dtype=jnp.int32)[None, :]).astype(BF)
    masked_query = dot(selector, query_states[0], 1, 0).astype(BF)
    packed = slabs_of(masked_query, key_states[0], value_states[0])
    heads_in = exchange(packed)
    masked_grad = dot(cot, out_weight, 1, 1).astype(BF)
    ring = (z + jnp.arange(4, dtype=jnp.int32)) % 4
    columns = ring * (2 * MSK)
    grads_out = pack_grads(ring * 640, masked_grad)
    own_grad = [grads_out[0]] + [move_z(grads_out[4 - dz], 4 - dz) for dz in (1, 2, 3)]
    own_all = jnp.concatenate(own_grad, axis=0)
    own_all, cot_got = lax.optimization_barrier((own_all, cot_got))
    got_grad = swap_y(
        jnp.concatenate(
            [lax.dynamic_slice_in_dim(own_all, (1 - y) * 384, 256, 1), own_all[:, 256:384]], axis=1
        )
    )
    place = jnp.concatenate([jnp.stack([y, 3 * y, 3 * y + 1, 0 * y + 2]), columns]).astype(jnp.int32)
    own_parts = [cot_kept] + [move_z(cot_kept, dz) for dz in (3, 2, 1)]
    other_parts = [cot_got] + [move_z(cot_got, dz) for dz in (3, 2, 1)]
    probs, att = forward(heads_in)
    att_got = swap_y(att[:256])
    place_back, own_parts = lax.optimization_barrier((place, own_parts))
    outs = backward(place_back, heads_in, own_grad, got_grad, probs, att)

    back = exchange(outs)
    own_parts, other_parts, att_got, _ = lax.optimization_barrier(
        (own_parts, other_parts, att_got, outs)
    )
    r = jnp.arange(640, dtype=jnp.int32)
    rc, rx, rl, rh, rr = r // 320, (r // 80) % 4, (r // 40) % 2, (r // 20) % 2, r % 20
    wanted = (
        ((y + rh) % 2) * 320
        + ((x + rx) % 4) * 80
        + ((low + rl) % 2) * 40
        + ((core + rc) % 2) * 20
        + rr
    )
    low_place = jnp.where(y == 0, wanted, wanted + 384)
    high_place = jnp.where(y == 0, wanted, wanted - 384)
    index = jnp.where(wanted < 256, low_place, jnp.where(wanted < 384, wanted, high_place))
    pick = (index[:, None] == r[None, :]).astype(BF)
    att_rows = (dot(pick[:, :SLAB], att, 1, 0) + dot(pick[:, SLAB:], att_got, 1, 0)).astype(BF)
    att_rows = lax.dynamic_slice_in_dim(
        jnp.concatenate([att_rows, att_rows], axis=1), z * 2 * MSK, QUERIES, 1
    )
    kept, sent = outer(place, att_rows, own_parts, other_parts)
    sent = swap_core(sent)
    chunks = [
        kept[i * 80 : (i + 1) * 80].astype(F32) + sent[i * 80 : (i + 1) * 80].astype(F32) for i in range(4)
    ]
    acc = chunks[0]
    for dx in (1, 2, 3):
        acc = acc + move_x(chunks[dx].astype(BF), dx).astype(F32)
    back, _ = lax.optimization_barrier((back, acc))
    quarter = acc.astype(BF)
    own_half = acc[:20] + move_y(quarter[40:60], 1, 0).astype(F32)
    other_half = move_y(quarter[20:40], 0, 1).astype(F32) + move_y(quarter[60:], 1, 1).astype(F32)
    weight_grad = jnp.where(
        y == 0,
        jnp.concatenate([own_half, other_half], axis=1),
        jnp.concatenate([other_half, own_half], axis=1),
    )

    grads = finish(back, selector)
    return (*(g[None] for g in grads), weight_grad)


def solution(mesh):
    return jax.shard_map(
        shards,
        mesh=mesh,
        in_specs=(
            P("dp", "blk", None),
            P("dp", "blk", None),
            P("dp", "blk", None),
            P("dp", "blk"),
            P("dp", "blk", None),
            P(),
        ),
        out_specs=(
            P("dp", "blk", None),
            P("dp", "blk", None),
            P("dp", "blk", None),
            P(("blk", "dp"), None),
        ),
        check_vma=False,
    )
```

```python
import math

import jax
import jax.numpy as jnp
from jax import lax
from jax.experimental import pallas as pl
from jax.experimental.pallas import tpu as pltpu
from jax.sharding import PartitionSpec as P

HEAD_DIM = 128
SCALE = 1.0 / math.sqrt(HEAD_DIM)
BF = jnp.bfloat16
F32 = jnp.float32
TOK = 128
MSK = 64
WIDTH = 2560
HEADS_DEV = 3
SLAB = HEADS_DEV * HEAD_DIM
QUERIES = 8 * MSK
KEYS = 8 * TOK
ROWS_OUT = MSK + 2 * TOK
ROWS_BACK = ROWS_OUT + 80
PARAMS = pltpu.CompilerParams(vmem_limit_bytes=40 * 2**20)


def exchange(a):
    return lax.all_to_all(a, "blk", 0, 0, tiled=True)


def move_x(a, dx):
    return lax.ppermute(a, "dp", [(i, (i + 4 * dx) % 16) for i in range(16)])


def move_y(a, dl, dh):
    pairs = []
    for i in range(128):
        b, d = i // 16, i % 16
        pairs.append((i, (b ^ dh) * 16 + (d ^ (2 * dl))))
    return lax.ppermute(a, ("blk", "dp"), pairs)


def move_z(a, dz):
    return lax.ppermute(a, "blk", [(i, (i + 2 * dz) % 8) for i in range(8)])


def swap_y(a):
    return lax.ppermute(a, "blk", [(i, i ^ 1) for i in range(8)])


def swap_core(a):
    return lax.ppermute(a, "dp", [(i, i ^ 1) for i in range(16)])


def dot(a, b, ca, cb):
    return lax.dot_general(a, b, (((ca,), (cb,)), ((), ())), preferred_element_type=F32)


def cost(flops, moved, exps=0):
    return pl.CostEstimate(flops=int(flops), bytes_accessed=int(moved), transcendentals=int(exps))


def slabs_of(query, key, value):
    def kernel(*refs):
        out_ref = refs[3]
        for j in range(8):
            pair = (j // 2) * 640 + (j % 2) * 384
            shared = (j // 2) * 640 + 256
            row = 0
            for ref in refs[:3]:
                at = pl.ds(row, ref.shape[0])
                out_ref[j, at, 0:256] = ref[:, pair : pair + 256]
                out_ref[j, at, 256:SLAB] = ref[:, shared : shared + HEAD_DIM]
                row += ref.shape[0]

    return pl.pallas_call(
        kernel,
        out_shape=jax.ShapeDtypeStruct((8, ROWS_OUT, SLAB), BF),
        compiler_params=PARAMS,
        cost_estimate=cost(0, ROWS_OUT * WIDTH * 4.4),
    )(query, key, value)


def pack_grads(starts, grad):
    def kernel(start_ref, grad_ref, *outs):
        for i, out_ref in enumerate(outs):
            out_ref[...] = grad_ref[:, pl.ds(pl.multiple_of(start_ref[i], HEAD_DIM), 640)]

    vmem = pl.BlockSpec(memory_space=pltpu.VMEM)
    return pl.pallas_call(
        kernel,
        in_specs=[pl.BlockSpec(memory_space=pltpu.SMEM), vmem],
        out_shape=[jax.ShapeDtypeStruct((MSK, 640), BF)] * 4,
        compiler_params=PARAMS,
        cost_estimate=cost(0, MSK * WIDTH * 4),
    )(starts, grad)


def outer(place, att_rows, own_parts, other_parts):
    width = other_parts[0].shape[1]
    rows = att_rows.shape[0] // 2
    tile = 1024

    def kernel(place_ref, att_ref, *refs):
        first = place_ref[0] == 0
        blocks = []
        for own, other in zip(refs[:4], refs[4:8]):
            blocks.append(jnp.where(first, own[...], other[...]))
            blocks.append(jnp.where(first, other[...], own[...]))
        cots = jnp.concatenate(blocks, axis=0)
        refs[8][...] = dot(att_ref[:rows], cots, 1, 0).astype(BF)
        refs[9][...] = dot(att_ref[rows:], cots, 1, 0).astype(BF)

    out = pl.BlockSpec((rows, tile), lambda i, *_: (0, i))
    return pl.pallas_call(
        kernel,
        grid_spec=pltpu.PrefetchScalarGridSpec(
            num_scalar_prefetch=1,
            grid=(width // tile,),
            in_specs=[pl.BlockSpec((2 * rows, QUERIES), lambda i, *_: (0, 0))]
            + [pl.BlockSpec((MSK, tile), lambda i, *_: (0, i))] * 8,
            out_specs=[out, out],
        ),
        out_shape=[
            pltpu.HBM((rows, width), BF),
            pltpu.HBM((rows, width), BF),
        ],
        compiler_params=PARAMS,
        cost_estimate=cost(1.4e9, 8e6),
    )(place, att_rows, *own_parts, *other_parts)


def finish(back, selector):
    def kernel(back_ref, selector_ref, query_ref, key_ref, value_ref):
        def put(to, query, key, value):
            query_ref[:, to] = dot(selector_ref[...], query, 0, 0).astype(BF)
            key_ref[:, to] = key
            value_ref[:, to] = value

        for j in range(8):
            at = (j // 2) * 640 + (j % 2) * 384
            put(
                slice(at, at + 256),
                back_ref[j, 0:MSK],
                back_ref[j, MSK : MSK + TOK],
                back_ref[j, MSK + TOK : ROWS_OUT],
            )
        for j in range(0, 8, 2):
            at = (j // 2) * 640 + 256
            halves = [
                jnp.concatenate(
                    [back_ref[k, ROWS_OUT:, 0:HEAD_DIM], back_ref[k, ROWS_OUT:, HEAD_DIM:]], axis=0
                )
                for k in (j, j + 1)
            ]
            query = jnp.concatenate([h[TOK:] for h in halves], axis=0)
            put(slice(at, at + HEAD_DIM), query, halves[0][0:TOK], halves[1][0:TOK])

    return pl.pallas_call(
        kernel,
        out_shape=[jax.ShapeDtypeStruct((TOK, WIDTH), BF)] * 3,
        compiler_params=PARAMS,
        cost_estimate=cost(2e10, 4e6),
    )(back, selector)


def forward_kernel(in_ref, prob_ref, att_ref):
    key = in_ref[:, MSK : MSK + TOK].reshape(KEYS, HEAD_DIM)
    value = in_ref[:, MSK + TOK :].reshape(KEYS, HEAD_DIM)
    query = in_ref[:, 0:MSK].reshape(QUERIES, HEAD_DIM)
    scores = dot(key, query, 1, 1) * SCALE
    top = jnp.max(scores, axis=0, keepdims=True)
    raised = jnp.exp(scores - top)
    total = jnp.sum(raised, axis=0, keepdims=True)
    probs = (raised * (1.0 / total)).astype(BF)
    prob_ref[0] = probs
    att_ref[...] = dot(value.T, probs, 1, 0).astype(BF)


def backward_kernel(place_ref, in_ref, *refs):
    own_refs, (got_ref, prob_ref, att_ref, out_ref, grad_ref) = refs[:4], refs[4:]
    key = in_ref[:, MSK : MSK + TOK].reshape(KEYS, HEAD_DIM)
    value = in_ref[:, MSK + TOK :].reshape(KEYS, HEAD_DIM)
    query = in_ref[:, 0:MSK].reshape(QUERIES, HEAD_DIM)
    for i in range(4):
        mine = pl.multiple_of(place_ref[4 + i] + place_ref[0] * MSK, MSK)
        other = pl.multiple_of(place_ref[4 + i] + (1 - place_ref[0]) * MSK, MSK)
        grad_ref[pl.ds(mine, MSK)] = own_refs[i][...]
        grad_ref[pl.ds(other, MSK)] = got_ref[i * MSK : (i + 1) * MSK]
    grad = grad_ref[...]
    delta = jnp.sum(grad.T.astype(F32) * att_ref[...].astype(F32), axis=0, keepdims=True)
    probs = prob_ref[0]
    prob_grad = dot(value, grad, 1, 1)
    score_grad = (probs.astype(F32) * (prob_grad - delta)).astype(BF)
    query_grad = (dot(key.T, score_grad, 1, 0) * SCALE).T.astype(BF)
    key_grad = (dot(score_grad, query, 1, 0) * SCALE).astype(BF)
    value_grad = dot(probs, grad, 1, 0).astype(BF)
    head = pl.program_id(0)
    query_grad = query_grad.reshape(8, MSK, HEAD_DIM)
    key_grad = key_grad.reshape(8, TOK, HEAD_DIM)
    value_grad = value_grad.reshape(8, TOK, HEAD_DIM)

    def own(at):
        out_ref[:, 0:MSK, at] = query_grad
        out_ref[:, MSK : MSK + TOK, at] = key_grad
        out_ref[:, MSK + TOK : ROWS_OUT, at] = value_grad

    @pl.when(head == 0)
    def _():
        own(slice(0, HEAD_DIM))

    @pl.when(head == 1)
    def _():
        own(slice(HEAD_DIM, 2 * HEAD_DIM))

    def half(grad, query):
        out_ref[:, ROWS_OUT:, 0:HEAD_DIM] = grad[:, 0:80]
        out_ref[:, ROWS_OUT : ROWS_OUT + 48, HEAD_DIM:] = grad[:, 80:]
        out_ref[:, ROWS_OUT + 48 :, HEAD_DIM:] = query

    @pl.when((head == 2) & (place_ref[0] == 0))
    def _():
        half(key_grad, query_grad[:, 0:32])

    @pl.when((head == 2) & (place_ref[0] == 1))
    def _():
        half(value_grad, query_grad[:, 32:])


def head_block(rows):
    return pl.BlockSpec((8, rows, HEAD_DIM), lambda h, *_: (0, 0, h))


PROB_BLOCK = pl.BlockSpec((1, KEYS, QUERIES), lambda h, *_: (h, 0, 0))
ATT_BLOCK = pl.BlockSpec((HEAD_DIM, QUERIES), lambda h, *_: (h, 0))


def forward(sent):
    return pl.pallas_call(
        forward_kernel,
        grid=(HEADS_DEV,),
        in_specs=[head_block(ROWS_OUT)],
        out_specs=[PROB_BLOCK, ATT_BLOCK],
        out_shape=[
            jax.ShapeDtypeStruct((HEADS_DEV, KEYS, QUERIES), BF),
            jax.ShapeDtypeStruct((SLAB, QUERIES), BF),
        ],
        compiler_params=PARAMS,
        cost_estimate=cost(1e6, 1e5),
    )(sent)


def backward(place, sent, own, got, probs, att):
    return pl.pallas_call(
        backward_kernel,
        grid_spec=pltpu.PrefetchScalarGridSpec(
            num_scalar_prefetch=1,
            grid=(HEADS_DEV,),
            in_specs=[
                head_block(ROWS_OUT),
                *[pl.BlockSpec((MSK, HEAD_DIM), lambda h, place: (0, place[1 + h]))] * 4,
                pl.BlockSpec((4 * MSK, HEAD_DIM), lambda h, *_: (0, h)),
                PROB_BLOCK,
                ATT_BLOCK,
            ],
            out_specs=pl.BlockSpec((8, ROWS_BACK, 2 * HEAD_DIM), lambda h, *_: (0, 0, 0)),
            scratch_shapes=[pltpu.VMEM((QUERIES, HEAD_DIM), BF)],
        ),
        out_shape=pltpu.HBM((8, ROWS_BACK, 2 * HEAD_DIM), BF),
        compiler_params=PARAMS,
        cost_estimate=cost(1e6, 1e5),
    )(place, sent, *own, got, probs, att)


def shards(query_states, key_states, value_states, mask_index, cotangent, out_weight):
    blk, dp = lax.axis_index("blk"), lax.axis_index("dp")
    z, y, core = blk // 2, blk % 2, dp % 2
    x, low = dp // 4, (dp // 2) % 2
    steps = mask_index[0] - blk * TOK

    cot = cotangent[0]
    half = cot.shape[1] // 2
    cot_kept = lax.dynamic_slice_in_dim(cot, y * half, half, 1)
    cot_got = swap_y(lax.dynamic_slice_in_dim(cot, (1 - y) * half, half, 1))
    selector = (steps[:, None] == jnp.arange(TOK, dtype=jnp.int32)[None, :]).astype(BF)
    masked_query = dot(selector, query_states[0], 1, 0).astype(BF)
    packed = slabs_of(masked_query, key_states[0], value_states[0])
    heads_in = exchange(packed)
    masked_grad = dot(cot, out_weight, 1, 1).astype(BF)
    ring = (z + jnp.arange(4, dtype=jnp.int32)) % 4
    columns = ring * (2 * MSK)
    grads_out = pack_grads(ring * 640, masked_grad)
    own_grad = [grads_out[0]] + [move_z(grads_out[4 - dz], 4 - dz) for dz in (1, 2, 3)]
    own_all = jnp.concatenate(own_grad, axis=0)
    r = jnp.arange(640, dtype=jnp.int32)
    rc, rx, rl, rh, rr = r // 320, (r // 80) % 4, (r // 40) % 2, (r // 20) % 2, r % 20
    wanted = (
        ((y + rh) % 2) * 320
        + ((x + rx) % 4) * 80
        + ((low + rl) % 2) * 40
        + ((core + rc) % 2) * 20
        + rr
    )
    low_place = jnp.where(y == 0, wanted, wanted + 384)
    high_place = jnp.where(y == 0, wanted, wanted - 384)
    index = jnp.where(wanted < 256, low_place, jnp.where(wanted < 384, wanted, high_place))
    pick = (index[:, None] == r[None, :]).astype(BF)
    own_all, cot_got, pick = lax.optimization_barrier((own_all, cot_got, pick))
    got_grad = swap_y(
        jnp.concatenate(
            [lax.dynamic_slice_in_dim(own_all, (1 - y) * 384, 256, 1), own_all[:, 256:384]], axis=1
        )
    )
    place = jnp.concatenate([jnp.stack([y, 3 * y, 3 * y + 1, 0 * y + 2]), columns]).astype(jnp.int32)
    own_parts = [cot_kept] + [move_z(cot_kept, dz) for dz in (3, 2, 1)]
    other_parts = [cot_got] + [move_z(cot_got, dz) for dz in (3, 2, 1)]
    probs, att = forward(heads_in)
    att_got = swap_y(att[:256])
    place_back, own_parts = lax.optimization_barrier((place, own_parts))
    outs = backward(place_back, heads_in, own_grad, got_grad, probs, att)

    back = exchange(outs)
    own_parts, other_parts, att_got, _ = lax.optimization_barrier(
        (own_parts, other_parts, att_got, outs)
    )
    att_rows = (dot(pick[:, :SLAB], att, 1, 0) + dot(pick[:, SLAB:], att_got, 1, 0)).astype(BF)
    att_rows = lax.dynamic_slice_in_dim(
        jnp.concatenate([att_rows, att_rows], axis=1), z * 2 * MSK, QUERIES, 1
    )
    kept, sent = outer(place, att_rows, own_parts, other_parts)
    sent = swap_core(sent)
    chunks = [
        kept[i * 80 : (i + 1) * 80].astype(F32) + sent[i * 80 : (i + 1) * 80].astype(F32) for i in range(4)
    ]
    acc = chunks[0]
    for dx in (1, 2, 3):
        acc = acc + move_x(chunks[dx].astype(BF), dx).astype(F32)
    back, _ = lax.optimization_barrier((back, acc))
    quarter = acc.astype(BF)
    own_half = acc[:20] + move_y(quarter[40:60], 1, 0).astype(F32)
    other_half = move_y(quarter[20:40], 0, 1).astype(F32) + move_y(quarter[60:], 1, 1).astype(F32)
    weight_grad = jnp.where(
        y == 0,
        jnp.concatenate([own_half, other_half], axis=1),
        jnp.concatenate([other_half, own_half], axis=1),
    )

    grads = finish(back, selector)
    return (*(g[None] for g in grads), weight_grad)


def solution(mesh):
    return jax.shard_map(
        shards,
        mesh=mesh,
        in_specs=(
            P("dp", "blk", None),
            P("dp", "blk", None),
            P("dp", "blk", None),
            P("dp", "blk"),
            P("dp", "blk", None),
            P(),
        ),
        out_specs=(
            P("dp", "blk", None),
            P("dp", "blk", None),
            P("dp", "blk", None),
            P(("blk", "dp"), None),
        ),
        check_vma=False,
    )
```
